32 devices in a mesh: groups: 2 (over y), space: 16 (over z, x, core).
Axes of the slice: x: 2, y: 2, z: 4, core: 2. Of those that a mesh axis runs over, the one named last changes fastest.
Arguments:
- video: bfloat16 [64, 16, 256, 256], P(None, None, ('groups', 'space')), parts along dimension 2, may hold values from -16 to 16
- shrink: float32 [2], P('groups'), parts along dimension 0, may hold values from 0.1 to 1
Outputs:
- denoised: bfloat16 [64, 16, 256, 256], P(None, None, ('groups', 'space')), parts along dimension 2
The draws below stay inside these ranges and needn't reach their ends.
There are 2 independent parts, one for each index of `groups`. The reference program is written for one: setup_inputs(seed, part) draws one part's arguments, and reference() takes and returns one part's arrays. A program takes and returns all parts, laid end to end along the dimension named above; each array names one. Nothing has to cross between parts.
All inputs are finite; a program needn't handle non-finite values.
Results may differ from the reference program's by a relative error of at most 0.001.
The reference program's roundings to bfloat16 on the way (of `filtered` and `mixing`) count: a program that leaves them out, or rounds other values in their place, can miss the bound.
Values may be sent and summed in bfloat16 or wider, within the bound.
A program may use at most 128 MiB of HBM per device.

```python
import math
import jax
import jax.numpy as jnp
from jax import lax

FRAMES = 64
Z = 16
X = 256
Y = 128


def draw_video(key, part):
    keys = jax.random.split(jax.random.fold_in(key, 71), 4)
    voxels = Z * Y * X
    temporal = jax.random.normal(keys[0], (8, FRAMES), jnp.float32)
    spatial = jax.random.normal(keys[1], (8, voxels), jnp.float32)
    strength = jnp.exp(jax.random.uniform(keys[2], (8, 1), jnp.float32, -0.7, 1.1))
    noise = jax.random.normal(keys[3], (FRAMES, voxels), jnp.float32)
    signal = jnp.dot((temporal * strength).T, spatial) / 3.0
    field = jnp.clip(signal + noise, -16.0, 16.0)
    return field.reshape(FRAMES, Z, Y, X).astype(jnp.bfloat16)


def setup_inputs(seed: int = 0, part: int = 0) -> dict:
    key_list = jax.random.split(jax.random.key(seed), 3)
    own_keys = jax.random.split(jax.random.fold_in(key_list[2], part), 3)
    return {
        "video": draw_video(jax.random.fold_in(jax.random.fold_in(key_list[2], part), 71), part),
        "shrink": jnp.clip(jnp.exp(jax.random.uniform(own_keys[1], (1,), jnp.float32, math.log(0.1), math.log(1.0))), 0.1, 1.0),
    }


def smooth_axis(field, axis):
    count = field.shape[axis]
    widths = [(0, 0)] * field.ndim
    widths[axis] = (1, 1)
    padded = jnp.pad(field, widths)
    lower = lax.slice_in_dim(padded, 0, count, axis=axis)
    middle = lax.slice_in_dim(padded, 1, count + 1, axis=axis)
    upper = lax.slice_in_dim(padded, 2, count + 2, axis=axis)
    return 0.25 * lower + 0.5 * middle + 0.25 * upper

def shrink_mixing(gram_sum, shrink):
    frames = gram_sum.shape[0]
    ridge = shrink[0] * jnp.trace(gram_sum) / frames
    system = gram_sum + ridge * jnp.eye(frames, dtype=jnp.float32)
    factor = jnp.linalg.cholesky(system)
    inner = lax.linalg.triangular_solve(factor, gram_sum, left_side=True, lower=True)
    mixing = lax.linalg.triangular_solve(factor, inner, left_side=True, lower=True, transpose_a=True)
    return mixing.astype(jnp.bfloat16)

def reference(video, shrink):
    values = video.astype(jnp.float32)
    smoothed = smooth_axis(smooth_axis(smooth_axis(values, 1), 2), 3)
    filtered = (values - smoothed).astype(jnp.bfloat16)
    flattened = filtered.reshape(filtered.shape[0], -1)
    gram_sum = jnp.dot(flattened.astype(jnp.float32), flattened.T.astype(jnp.float32), preferred_element_type=jnp.float32)
    mixing = shrink_mixing(gram_sum, shrink)
    result = jnp.dot(mixing.T.astype(jnp.float32), flattened.astype(jnp.float32), preferred_element_type=jnp.float32)
    return result.astype(jnp.bfloat16).reshape(video.shape)
```

```python
import functools

import jax
import jax.numpy as jnp
from jax import lax
from jax.experimental import pallas as pl
from jax.experimental.pallas import tpu as pltpu
from jax.sharding import PartitionSpec as P

MESH = pl.DeviceIdType.MESH
F32 = jnp.float32
BF16 = jnp.bfloat16


def iota(shape, dim):
    return lax.broadcasted_iota(jnp.int32, shape, dim)


def dot(a, b):
    return jnp.dot(a, b, preferred_element_type=F32)


def chunk_bounds(depth, chunks):
    return [depth * c // chunks for c in range(chunks + 1)]


def filter_kernel(
    cfg, video, flat, gram_out,
    vid, abf, part, send, recv, fbuf, mat, gsend, grecv1, grecv2,
    load_sem, store_sem, hsend_sem, hrecv_sem, g1s_sem, g1r_sem, g2s_sem, g2r_sem,
):
    n, inner, outer, frames, depth, rows, width, block, chunks = cfg
    me = lax.axis_index("space")
    bounds = chunk_bounds(depth, chunks)
    total = frames * rows
    blocks = total // block
    fb = block // rows
    has_prev, has_next = me > 0, me < n - 1

    loads = []
    for c in range(chunks):
        zs = pl.ds(bounds[c], bounds[c + 1] - bounds[c])
        loads.append(pltpu.make_async_copy(video.at[:, zs], vid.at[:, zs], load_sem.at[c]))
        loads[-1].start()

    pos, ring = lax.rem(me, inner), me // inner
    peers1 = [ring * inner + lax.rem(pos + d, inner) for d in range(1, inner)]
    peers2 = [lax.rem(ring + d, outer) * inner + pos for d in range(1, outer)]
    barrier = pltpu.get_barrier_semaphore()

    @pl.when(has_prev)
    def _():
        pl.semaphore_signal(barrier, inc=1, device_id={"space": me - 1}, device_id_type=MESH)

    @pl.when(has_next)
    def _():
        pl.semaphore_signal(barrier, inc=1, device_id={"space": me + 1}, device_id_type=MESH)

    for peer in peers1 + peers2:
        pl.semaphore_signal(barrier, inc=1, device_id={"space": peer}, device_id_type=MESH)

    r, c = iota((block, block), 0), iota((block, block), 1)
    same = (r // rows) == (c // rows)
    step = r - c
    tri = jnp.where(step == 0, 2.0, jnp.where((step == 1) | (step == -1), 1.0, 0.0))
    tri = jnp.where(same, tri, 0.0) / 64.0
    weights = jnp.concatenate([tri, 2.0 * tri, tri], axis=1).astype(BF16)
    r, c = iota((2 * fb, block), 0), iota((2 * fb, block), 1)
    wanted = jnp.where(r < fb, r * rows, (r - fb) * rows + rows - 1)
    pick = jnp.where(wanted == c, 1.0, 0.0).astype(BF16)
    r, c = iota((block, 6 * fb), 0), iota((block, 6 * fb), 1)
    side, zstep = c // (3 * fb), lax.rem(c // fb, 3)
    target = lax.rem(c, fb) * rows + side * (rows - 1)
    hweights = jnp.where(r == target, jnp.where(zstep == 1, 2.0, 1.0), 0.0) / 64.0
    hweights = hweights.astype(BF16)

    zero = jnp.zeros((total, width), BF16)
    abf[0] = zero
    abf[depth + 1] = zero
    for s in range(2):
        recv[s, 0] = jnp.zeros((frames, width), BF16)
        recv[s, depth + 1] = jnp.zeros((frames, width), BF16)

    @pl.when(jnp.logical_not(has_prev))
    def _():
        recv[0] = jnp.zeros((depth + 2, frames, width), BF16)

    @pl.when(jnp.logical_not(has_next))
    def _():
        recv[1] = jnp.zeros((depth + 2, frames, width), BF16)

    def halo(side, c):
        count = bounds[c + 1] - bounds[c]
        return pltpu.make_async_remote_copy(
            src_ref=send.at[side, pl.ds(bounds[c], count)],
            dst_ref=recv.at[side, pl.ds(bounds[c] + 1, count)],
            send_sem=hsend_sem.at[side, c],
            recv_sem=hrecv_sem.at[side, c],
            device_id={"space": me + 1 if side == 0 else me - 1},
            device_id_type=MESH,
        )

    for c in range(chunks):
        loads[c].wait()

        def take(z, carry):
            full = vid[:, z].astype(F32).reshape(total, width).astype(BF16)
            abf[z + 1] = full
            for b in range(blocks):
                ends = dot(pick, full[b * block:(b + 1) * block]).astype(BF16)
                send[1, z, b * fb:(b + 1) * fb] = ends[:fb]
                send[0, z, b * fb:(b + 1) * fb] = ends[fb:]
            return carry

        lax.fori_loop(bounds[c], bounds[c + 1], take, 0)
        if c == 0:
            waits = has_prev.astype(jnp.int32) + has_next.astype(jnp.int32)
            pl.semaphore_wait(barrier, waits + (inner - 1) + (outer - 1))

        @pl.when(has_next)
        def _():
            halo(0, c).start()

        @pl.when(has_prev)
        def _():
            halo(1, c).start()

    def inside(z, carry):
        for b in range(blocks):
            stack = abf[pl.ds(z, 3), b * block:(b + 1) * block].reshape(3 * block, width)
            part[z, b * block:(b + 1) * block] = dot(weights, stack)
        return carry

    lax.fori_loop(0, depth, inside, 0)

    lane = iota((block, width), 1)
    stores = []
    for c in range(chunks):
        @pl.when(has_prev)
        def _():
            halo(0, c).wait_recv()

        @pl.when(has_next)
        def _():
            halo(1, c).wait_recv()

        lo = bounds[c] - 1 if c else 0
        hi = bounds[c + 1] - 1 if c < chunks - 1 else depth

        def finish(z, carry):
            columns = pl.ds(pl.multiple_of(z * width, width), width)
            for b in range(blocks):
                mine = slice(b * block, (b + 1) * block)
                ours = slice(b * fb, (b + 1) * fb)
                above = recv[0, pl.ds(z, 3), ours].reshape(3 * fb, width)
                below = recv[1, pl.ds(z, 3), ours].reshape(3 * fb, width)
                near = part[z, mine] + dot(hweights, jnp.concatenate([above, below], axis=0))
                left = jnp.where(lane == 0, 0.0, pltpu.roll(near, 1, 1))
                right = jnp.where(lane == width - 1, 0.0, pltpu.roll(near, width - 1, 1))
                smooth = (left + right) + 2.0 * near
                fbuf[mine, columns] = (abf[z + 1, mine].astype(F32) - smooth).astype(BF16)
            return carry

        lax.fori_loop(lo, hi, finish, 0)
        cols = pl.ds(lo * width, (hi - lo) * width)
        stores.append(pltpu.make_async_copy(fbuf.at[:, cols], flat.at[:, cols], store_sem.at[c]))
        stores[-1].start()
        for i in range(blocks):
            for j in range(blocks):
                ri, rj = slice(i * block, (i + 1) * block), slice(j * block, (j + 1) * block)
                value = lax.dot_general(
                    fbuf[ri, cols], fbuf[rj, cols], (((1,), (1,)), ((), ())),
                    preferred_element_type=F32,
                )
                mat[ri, rj] = value if c == 0 else mat[ri, rj] + value

    keep = lax.rem(iota((total, total), 0), rows) == lax.rem(iota((total, total), 1), rows)
    kept = jnp.where(keep, mat[...], 0.0)
    summed = jnp.sum(kept.reshape(frames, rows, total), axis=1)
    half = frames // 2
    r, c = iota((total, 2 * frames), 0), iota((total, 2 * frames), 1)
    gather_l = jnp.where(r // rows == c, 1.0, 0.0)
    gather_r = jnp.where(r // rows == c - frames, 1.0, 0.0)
    hp = functools.partial(jnp.dot, preferred_element_type=F32, precision=lax.Precision.HIGHEST)
    packed = hp(summed[:half], gather_l) + hp(summed[half:], gather_r)

    def exchange(value, slot, peers, recv_ref, ssem, rsem):
        gsend[slot] = value
        copies = []
        for d, peer in enumerate(peers):
            copies.append(pltpu.make_async_remote_copy(
                src_ref=gsend.at[slot], dst_ref=recv_ref.at[d],
                send_sem=ssem.at[d], recv_sem=rsem.at[d],
                device_id={"space": peer}, device_id_type=MESH,
            ))
            copies[-1].start()
        for d, copy in enumerate(copies):
            copy.wait_recv()
            value = value + recv_ref[d]
        return value, copies

    packed, copies1 = exchange(packed, 0, peers1, grecv1, g1s_sem, g1r_sem)
    packed, copies2 = exchange(packed, 1, peers2, grecv2, g2s_sem, g2r_sem)
    gram_out[...] = packed
    for copy in copies1 + copies2:
        copy.wait_send()
    for c in range(chunks):
        @pl.when(has_next)
        def _():
            halo(0, c).wait_send()

        @pl.when(has_prev)
        def _():
            halo(1, c).wait_send()
    for store in stores:
        store.wait()


def filtered_gram(video, n):
    frames, depth, rows, width = video.shape
    total = frames * rows
    block = min(total, max(rows, (256 // rows) * rows))
    chunks = 4 if depth % 4 == 0 else 1
    inner = 4 if n % 4 == 0 else (2 if n % 2 == 0 else 1)
    outer = n // inner
    cfg = (n, inner, outer, frames, depth, rows, width, block, chunks)
    half = frames // 2
    dma = pltpu.SemaphoreType.DMA
    return pl.pallas_call(
        functools.partial(filter_kernel, cfg),
        out_shape=(
            jax.ShapeDtypeStruct((total, depth * width), BF16),
            jax.ShapeDtypeStruct((half, 2 * frames), F32),
        ),
        in_specs=[pl.BlockSpec(memory_space=pl.ANY)],
        out_specs=(
            pl.BlockSpec(memory_space=pl.ANY),
            pl.BlockSpec(memory_space=pltpu.VMEM),
        ),
        scratch_shapes=[
            pltpu.VMEM((frames, depth, rows, width), BF16),
            pltpu.VMEM((depth + 2, total, width), BF16),
            pltpu.VMEM((depth, total, width), F32),
            pltpu.VMEM((2, depth, frames, width), BF16),
            pltpu.VMEM((2, depth + 2, frames, width), BF16),
            pltpu.VMEM((total, depth * width), BF16),
            pltpu.VMEM((total, total), F32),
            pltpu.VMEM((2, half, 2 * frames), F32),
            pltpu.VMEM((max(inner - 1, 1), half, 2 * frames), F32),
            pltpu.VMEM((max(outer - 1, 1), half, 2 * frames), F32),
            dma((chunks,)),
            dma((chunks,)),
            dma((2, chunks)),
            dma((2, chunks)),
            dma((max(inner - 1, 1),)),
            dma((max(inner - 1, 1),)),
            dma((max(outer - 1, 1),)),
            dma((max(outer - 1, 1),)),
        ],
        compiler_params=pltpu.CompilerParams(
            collective_id=0, has_side_effects=True, vmem_limit_bytes=48 * 2**20
        ),
    )(video)


def remix_kernel(cfg, shrink, gram, flat, out, fbuf, obuf, load_sem, store_sem):
    frames, depth, rows, width, chunks = cfg
    bounds = chunk_bounds(depth, chunks)
    total, half, lanes = frames * rows, frames // 2, 2 * frames
    loads = []
    for c in range(chunks):
        cols = pl.ds(bounds[c] * width, (bounds[c + 1] - bounds[c]) * width)
        loads.append(pltpu.make_async_copy(flat.at[:, cols], fbuf.at[:, cols], load_sem.at[c]))
        loads[-1].start()

    packed = gram[...]
    other = pltpu.roll(packed, frames, 1)
    r, c = iota((frames, lanes), 0), iota((frames, lanes), 1)
    whole = jnp.where(c < frames, jnp.concatenate([packed, other], axis=0), 0.0)
    eye = jnp.where(r == c, 1.0, 0.0)
    ridge = shrink[0] * jnp.sum(whole * eye) / frames
    system = whole + ridge * eye

    tiles = frames // 8
    parts = [system[8 * t:8 * t + 8] for t in range(tiles)]
    lane, sub = iota((8, lanes), 1), iota((8, lanes), 0)
    for k in range(frames):
        home, at = k // 8, k % 8
        cols = [jnp.broadcast_to(p[:, k:k + 1], (8, lanes)) for p in parts]
        row = jnp.broadcast_to(parts[home][at:at + 1], (8, lanes))
        inverse = 1.0 / jnp.broadcast_to(cols[home][at:at + 1], (8, lanes))
        scaled = row * inverse
        for t in range(tiles):
            new = jnp.where(lane == k, cols[t] * inverse, parts[t] - cols[t] * scaled)
            if t == home:
                new = jnp.where(sub == at, jnp.where(lane == k, -inverse, scaled), new)
            parts[t] = new
    mixing = (eye + ridge * jnp.concatenate(parts, axis=0)).astype(BF16)

    r, c = iota((total, frames), 0), iota((total, frames), 1)
    spread = jnp.where(r // rows == c, 1.0, 0.0).astype(BF16)
    tall = dot(spread, mixing).astype(BF16)
    r, c = iota((lanes, total), 0), iota((lanes, total), 1)
    spread = jnp.where(r == c // rows, 1.0, 0.0).astype(BF16)
    big = dot(tall, spread)
    keep = lax.rem(iota((total, total), 0), rows) == lax.rem(iota((total, total), 1), rows)
    big = jnp.where(keep, big, 0.0).astype(BF16)

    stores = []
    for c in range(chunks):
        loads[c].wait()

        def mix(z, carry):
            columns = pl.ds(pl.multiple_of(z * width, width), width)
            value = dot(big, fbuf[:, columns])
            obuf[:, z] = value.reshape(frames, rows, width).astype(BF16)
            return carry

        lax.fori_loop(bounds[c], bounds[c + 1], mix, 0)
        zs = pl.ds(bounds[c], bounds[c + 1] - bounds[c])
        stores.append(pltpu.make_async_copy(obuf.at[:, zs], out.at[:, zs], store_sem.at[c]))
        stores[-1].start()
    for store in stores:
        store.wait()


def remix(shrink, gram, flat, shape):
    frames, depth, rows, width = shape
    chunks = 4 if depth % 4 == 0 else 1
    cfg = (frames, depth, rows, width, chunks)
    return pl.pallas_call(
        functools.partial(remix_kernel, cfg),
        out_shape=jax.ShapeDtypeStruct(shape, BF16),
        in_specs=[
            pl.BlockSpec(memory_space=pltpu.SMEM),
            pl.BlockSpec(memory_space=pltpu.VMEM),
            pl.BlockSpec(memory_space=pl.ANY),
        ],
        out_specs=pl.BlockSpec(memory_space=pl.ANY),
        scratch_shapes=[
            pltpu.VMEM((frames * rows, depth * width), BF16),
            pltpu.VMEM(shape, BF16),
            pltpu.SemaphoreType.DMA((chunks,)),
            pltpu.SemaphoreType.DMA((chunks,)),
        ],
        compiler_params=pltpu.CompilerParams(vmem_limit_bytes=32 * 2**20),
    )(shrink, gram, flat)


def per_device(n, video, shrink):
    flat, gram = filtered_gram(video, n)
    return remix(shrink, gram, flat, video.shape)


def solution(mesh):
    return jax.shard_map(
        functools.partial(per_device, mesh.shape["space"]),
        mesh=mesh,
        in_specs=(P(None, None, ("groups", "space"), None), P("groups")),
        out_specs=P(None, None, ("groups", "space"), None),
        check_vma=False,
    )
```

```python
import functools

import jax
import jax.numpy as jnp
from jax import lax
from jax.experimental import pallas as pl
from jax.experimental.pallas import tpu as pltpu
from jax.sharding import PartitionSpec as P

MESH = pl.DeviceIdType.MESH
F32 = jnp.float32
BF16 = jnp.bfloat16


def iota(shape, dim):
    return lax.broadcasted_iota(jnp.int32, shape, dim)


def dot(a, b):
    return jnp.dot(a, b, preferred_element_type=F32)


def chunk_bounds(depth, chunks):
    return [depth * c // chunks for c in range(chunks + 1)]


def filter_kernel(
    cfg, video, flat, gram_out,
    vid, vox, zsum, recv, acc, gsend, grecv1, grecv2,
    load_sem, hsend_sem, hrecv_sem, g1s_sem, g1r_sem, g2s_sem, g2r_sem,
):
    n, inner, outer, frames, depth, rows, width, block, chunks = cfg
    me = lax.axis_index("space")
    bounds = chunk_bounds(depth, chunks)
    total = frames * rows
    blocks = total // block
    fb = block // rows
    has_prev, has_next = me > 0, me < n - 1

    loads = []
    for c in range(chunks):
        zs = pl.ds(bounds[c], bounds[c + 1] - bounds[c])
        loads.append(pltpu.make_async_copy(video.at[:, zs], vid.at[:, zs], load_sem.at[c]))
        loads[-1].start()

    pos, ring = lax.rem(me, inner), me // inner
    peers1 = [ring * inner + lax.rem(pos + d, inner) for d in range(1, inner)]
    peers2 = [lax.rem(ring + d, outer) * inner + pos for d in range(1, outer)]
    barrier = pltpu.get_barrier_semaphore()

    @pl.when(has_prev)
    def _():
        pl.semaphore_signal(barrier, inc=1, device_id={"space": me - 1}, device_id_type=MESH)

    @pl.when(has_next)
    def _():
        pl.semaphore_signal(barrier, inc=1, device_id={"space": me + 1}, device_id_type=MESH)

    for peer in peers1 + peers2:
        pl.semaphore_signal(barrier, inc=1, device_id={"space": peer}, device_id_type=MESH)

    r, c = iota((block, block), 0), iota((block, block), 1)
    turn = jnp.where(lax.rem(r, fb) * rows + r // fb == c, 1.0, 0.0).astype(BF16)
    r, c = iota((width, width), 0), iota((width, width), 1)
    step = r - c
    along = jnp.where(step == 0, 2.0, jnp.where((step == 1) | (step == -1), 1.0, 0.0))
    along = (along / 64.0).astype(BF16)

    zero = jnp.zeros((frames, width), BF16)
    for y in range(rows):
        vox[y, 0] = zero
        vox[y, depth + 1] = zero
    for s in range(2):
        recv[s, 0] = zero
        recv[s, depth + 1] = zero

    @pl.when(jnp.logical_not(has_prev))
    def _():
        recv[0] = jnp.zeros((depth + 2, frames, width), BF16)

    @pl.when(jnp.logical_not(has_next))
    def _():
        recv[1] = jnp.zeros((depth + 2, frames, width), BF16)

    def halo(side, c):
        zs = pl.ds(bounds[c] + 1, bounds[c + 1] - bounds[c])
        return pltpu.make_async_remote_copy(
            src_ref=vox.at[rows - 1 if side == 0 else 0, zs],
            dst_ref=recv.at[side, zs],
            send_sem=hsend_sem.at[side, c],
            recv_sem=hrecv_sem.at[side, c],
            device_id={"space": me + 1 if side == 0 else me - 1},
            device_id_type=MESH,
        )

    for c in range(chunks):
        loads[c].wait()

        def take(z, carry):
            full = vid[:, z].astype(F32).reshape(total, width).astype(BF16)
            for b in range(blocks):
                turned = dot(turn, full[b * block:(b + 1) * block]).astype(BF16)
                for y in range(rows):
                    vox[y, z + 1, b * fb:(b + 1) * fb] = turned[y * fb:(y + 1) * fb]
            return carry

        lax.fori_loop(bounds[c], bounds[c + 1], take, 0)
        if c == 0:
            waits = has_prev.astype(jnp.int32) + has_next.astype(jnp.int32)
            pl.semaphore_wait(barrier, waits + (inner - 1) + (outer - 1))

        @pl.when(has_next)
        def _():
            halo(0, c).start()

        @pl.when(has_prev)
        def _():
            halo(1, c).start()

    def smooth_xz(field):
        flatter = field.reshape((depth + 2) * frames, width)
        x = dot(flatter, along).reshape(depth + 2, frames, width)
        return (x[:depth] + x[2:]) + 2.0 * x[1:depth + 1]

    def first(y, carry):
        zsum[y] = smooth_xz(vox[y])
        return carry

    lax.fori_loop(0, rows, first, 0)

    def place(slot, y, smooth):
        high = (vox[y, pl.ds(1, depth)].astype(F32) - smooth).astype(BF16)
        base = slot * frames
        if not isinstance(slot, int):
            base = pl.multiple_of(base, frames)
        for z in range(depth):
            flat[pl.ds(base, frames), z * width:(z + 1) * width] = high[z]

    def inside(y, carry):
        place(y - 1, y, (zsum[y - 1] + zsum[y + 1]) + 2.0 * zsum[y])
        return carry

    lax.fori_loop(1, rows - 1, inside, 0)

    def gram_of(pair):
        base = pair * 2 * frames
        if not isinstance(pair, int):
            base = pl.multiple_of(base, 2 * frames)
        both = flat[pl.ds(base, 2 * frames), :]
        return lax.dot_general(
            both, both, (((1,), (1,)), ((), ())), preferred_element_type=F32
        )

    acc[...] = jnp.zeros_like(acc)

    def add_gram(pair, carry):
        acc[...] += gram_of(pair)
        return carry

    lax.fori_loop(0, rows // 2 - 1, add_gram, 0)

    for c in range(chunks):
        @pl.when(has_next)
        def _():
            halo(1, c).wait_recv()
    place(rows - 2, rows - 1, (zsum[rows - 2] + smooth_xz(recv[1])) + 2.0 * zsum[rows - 1])
    for c in range(chunks):
        @pl.when(has_prev)
        def _():
            halo(0, c).wait_recv()
    place(rows - 1, 0, (smooth_xz(recv[0]) + zsum[1]) + 2.0 * zsum[0])

    half = frames // 2
    pairs = acc[...] + gram_of(rows // 2 - 1)
    whole = pairs[:frames] + pltpu.roll(pairs[frames:], frames, 1)
    whole = jnp.where(iota((frames, 2 * frames), 1) < frames, whole, 0.0)
    packed = whole[:half] + pltpu.roll(whole[half:], frames, 1)

    def exchange(value, slot, peers, recv_ref, ssem, rsem):
        gsend[slot] = value
        copies = []
        for d, peer in enumerate(peers):
            copies.append(pltpu.make_async_remote_copy(
                src_ref=gsend.at[slot], dst_ref=recv_ref.at[d],
                send_sem=ssem.at[d], recv_sem=rsem.at[d],
                device_id={"space": peer}, device_id_type=MESH,
            ))
            copies[-1].start()
        for d, copy in enumerate(copies):
            copy.wait_recv()
            value = value + recv_ref[d]
        return value, copies

    packed, copies1 = exchange(packed, 0, peers1, grecv1, g1s_sem, g1r_sem)
    packed, copies2 = exchange(packed, 1, peers2, grecv2, g2s_sem, g2r_sem)
    gram_out[...] = packed
    for copy in copies1 + copies2:
        copy.wait_send()
    for c in range(chunks):
        @pl.when(has_next)
        def _():
            halo(0, c).wait_send()

        @pl.when(has_prev)
        def _():
            halo(1, c).wait_send()


def filtered_gram(video, n):
    frames, depth, rows, width = video.shape
    total = frames * rows
    block = min(total, max(rows, (256 // rows) * rows))
    chunks = 4 if depth % 4 == 0 else 1
    inner = 4 if n % 4 == 0 else (2 if n % 2 == 0 else 1)
    outer = n // inner
    cfg = (n, inner, outer, frames, depth, rows, width, block, chunks)
    half = frames // 2
    dma = pltpu.SemaphoreType.DMA
    return pl.pallas_call(
        functools.partial(filter_kernel, cfg),
        out_shape=(
            jax.ShapeDtypeStruct((total, depth * width), BF16),
            jax.ShapeDtypeStruct((half, 2 * frames), F32),
        ),
        in_specs=[pl.BlockSpec(memory_space=pl.ANY)],
        out_specs=(
            pl.BlockSpec(memory_space=pltpu.VMEM),
            pl.BlockSpec(memory_space=pltpu.VMEM),
        ),
        scratch_shapes=[
            pltpu.VMEM((frames, depth, rows, width), BF16),
            pltpu.VMEM((rows, depth + 2, frames, width), BF16),
            pltpu.VMEM((rows, depth, frames, width), F32),
            pltpu.VMEM((2, depth + 2, frames, width), BF16),
            pltpu.VMEM((2 * frames, 2 * frames), F32),
            pltpu.VMEM((2, half, 2 * frames), F32),
            pltpu.VMEM((max(inner - 1, 1), half, 2 * frames), F32),
            pltpu.VMEM((max(outer - 1, 1), half, 2 * frames), F32),
            dma((chunks,)),
            dma((2, chunks)),
            dma((2, chunks)),
            dma((max(inner - 1, 1),)),
            dma((max(inner - 1, 1),)),
            dma((max(outer - 1, 1),)),
            dma((max(outer - 1, 1),)),
        ],
        compiler_params=pltpu.CompilerParams(
            collective_id=0, has_side_effects=True, vmem_limit_bytes=48 * 2**20
        ),
    )(video)


def remix_kernel(cfg, shrink, gram, flat, out, obuf, store_sem):
    frames, depth, rows, width, chunks = cfg
    bounds = chunk_bounds(depth, chunks)
    total, half, lanes = frames * rows, frames // 2, 2 * frames
    packed = gram[...]
    other = pltpu.roll(packed, frames, 1)
    r, c = iota((frames, lanes), 0), iota((frames, lanes), 1)
    whole = jnp.where(c < frames, jnp.concatenate([packed, other], axis=0), 0.0)
    eye = jnp.where(r == c, 1.0, 0.0)
    ridge = shrink[0] * jnp.sum(whole * eye) / frames
    system = whole + ridge * eye

    tiles = frames // 8
    parts = [system[8 * t:8 * t + 8] for t in range(tiles)]
    lane, sub = iota((8, lanes), 1), iota((8, lanes), 0)
    group = 4
    for k in range(0, frames, group):
        home, at = k // 8, k % 8
        span = range(group)
        cols = [[jnp.broadcast_to(p[:, k + i:k + i + 1], (8, lanes)) for p in parts] for i in span]
        line = [jnp.broadcast_to(parts[home][at + i:at + i + 1], (8, lanes)) for i in span]
        own = {}
        for i in span:
            for j in range(i + 1):
                own[i, j] = jnp.broadcast_to(cols[j][home][at + i:at + i + 1], (8, lanes))

        def of(i, j):
            return own[max(i, j), min(i, j)]

        for q in span:
            inverse = 1.0 / own[q, q]
            scaled = [of(i, q) * inverse for i in span]
            fresh = {}
            for i in span:
                for j in range(i + 1):
                    if i == q and j == q:
                        fresh[i, j] = -inverse
                    elif i == q:
                        fresh[i, j] = scaled[j]
                    elif j == q:
                        fresh[i, j] = scaled[i]
                    else:
                        fresh[i, j] = own[i, j] - of(i, q) * scaled[j]
            own = fresh
        wide = []
        for i in span:
            value = -sum(of(i, j) * line[j] for j in span)
            for j in span:
                value = jnp.where(lane == k + j, of(i, j), value)
            wide.append(value)
        inside = (lane >= k) & (lane < k + group)
        for t in range(tiles):
            terms = [cols[i][t] * wide[i] for i in span]
            while len(terms) > 1:
                terms = [a + b for a, b in zip(terms[::2], terms[1::2])]
            new = jnp.where(inside, 0.0, parts[t]) - terms[0]
            if t == home:
                for i in span:
                    new = jnp.where(sub == at + i, wide[i], new)
            parts[t] = new
    mixing = (eye + ridge * jnp.concatenate(parts, axis=0)).astype(BF16)

    r, c = iota((total, frames), 0), iota((total, frames), 1)
    spread = jnp.where(r // rows == c, 1.0, 0.0).astype(BF16)
    tall = dot(spread, mixing).astype(BF16)
    r, c = iota((lanes, total), 0), iota((lanes, total), 1)
    spread = jnp.where(r == lax.rem(c, frames), 1.0, 0.0).astype(BF16)
    big = dot(tall, spread)
    keep = lax.rem(iota((total, total), 0), rows) == lax.rem(iota((total, total), 1) // frames + 1, rows)
    big = jnp.where(keep, big, 0.0).astype(BF16)

    stores = []
    for c in range(chunks):
        def mix(z, carry):
            columns = pl.ds(pl.multiple_of(z * width, width), width)
            value = dot(big, flat[:, columns])
            obuf[:, z] = value.reshape(frames, rows, width).astype(BF16)
            return carry

        lax.fori_loop(bounds[c], bounds[c + 1], mix, 0)
        zs = pl.ds(bounds[c], bounds[c + 1] - bounds[c])
        stores.append(pltpu.make_async_copy(obuf.at[:, zs], out.at[:, zs], store_sem.at[c]))
        stores[-1].start()
    for store in stores:
        store.wait()


def remix(shrink, gram, flat, shape):
    frames, depth, rows, width = shape
    chunks = 4 if depth % 4 == 0 else 1
    cfg = (frames, depth, rows, width, chunks)
    return pl.pallas_call(
        functools.partial(remix_kernel, cfg),
        out_shape=jax.ShapeDtypeStruct(shape, BF16),
        in_specs=[
            pl.BlockSpec(memory_space=pltpu.SMEM),
            pl.BlockSpec(memory_space=pltpu.VMEM),
            pl.BlockSpec(memory_space=pltpu.VMEM),
        ],
        out_specs=pl.BlockSpec(memory_space=pl.ANY),
        scratch_shapes=[
            pltpu.VMEM(shape, BF16),
            pltpu.SemaphoreType.DMA((chunks,)),
        ],
        compiler_params=pltpu.CompilerParams(vmem_limit_bytes=32 * 2**20),
    )(shrink, gram, flat)


def per_device(n, video, shrink):
    flat, gram = filtered_gram(video, n)
    return remix(shrink, gram, flat, video.shape)


def solution(mesh):
    return jax.shard_map(
        functools.partial(per_device, mesh.shape["space"]),
        mesh=mesh,
        in_specs=(P(None, None, ("groups", "space"), None), P("groups")),
        out_specs=P(None, None, ("groups", "space"), None),
        check_vma=False,
    )
```

```python
import functools

import jax
import jax.numpy as jnp
from jax import lax
from jax.experimental import pallas as pl
from jax.experimental.pallas import tpu as pltpu
from jax.sharding import PartitionSpec as P

MESH = pl.DeviceIdType.MESH
F32 = jnp.float32
BF16 = jnp.bfloat16


def iota(shape, dim):
    return lax.broadcasted_iota(jnp.int32, shape, dim)


def recip(x):
    r = pl.reciprocal(x, approx=True)
    for _ in range(2):
        r = r * (2.0 - x * r)
    return r


def dot(a, b):
    return jnp.dot(a, b, preferred_element_type=F32)


def chunk_bounds(depth, chunks):
    return [depth * c // chunks for c in range(chunks + 1)]


def filter_kernel(
    cfg, video, flat, gram_out,
    vid, vox, zsum, recv, acc, gsend, grecv1, grecv2,
    load_sem, hsend_sem, hrecv_sem, g1s_sem, g1r_sem, g2s_sem, g2r_sem,
):
    n, inner, outer, frames, depth, rows, width, block, chunks = cfg
    me = lax.axis_index("space")
    bounds = chunk_bounds(depth, chunks)
    total = frames * rows
    blocks = total // block
    fb = block // rows
    has_prev, has_next = me > 0, me < n - 1

    loads = []
    for c in range(chunks):
        zs = pl.ds(bounds[c], bounds[c + 1] - bounds[c])
        loads.append(pltpu.make_async_copy(video.at[:, zs], vid.at[:, zs], load_sem.at[c]))
        loads[-1].start()

    pos, ring = lax.rem(me, inner), me // inner
    peers1 = [ring * inner + lax.rem(pos + d, inner) for d in range(1, inner)]
    peers2 = [lax.rem(ring + d, outer) * inner + pos for d in range(1, outer)]
    barrier = pltpu.get_barrier_semaphore()

    @pl.when(has_prev)
    def _():
        pl.semaphore_signal(barrier, inc=1, device_id={"space": me - 1}, device_id_type=MESH)

    @pl.when(has_next)
    def _():
        pl.semaphore_signal(barrier, inc=1, device_id={"space": me + 1}, device_id_type=MESH)

    for peer in peers1 + peers2:
        pl.semaphore_signal(barrier, inc=1, device_id={"space": peer}, device_id_type=MESH)

    r, c = iota((block, block), 0), iota((block, block), 1)
    turn = jnp.where(lax.rem(r, fb) * rows + r // fb == c, 1.0, 0.0).astype(BF16)
    r, c = iota((width, width), 0), iota((width, width), 1)
    step = r - c
    along = jnp.where(step == 0, 2.0, jnp.where((step == 1) | (step == -1), 1.0, 0.0))
    along = (along / 64.0).astype(BF16)

    zero = jnp.zeros((frames, width), BF16)
    for y in range(rows):
        vox[y, 0] = zero
        vox[y, depth + 1] = zero
    for s in range(2):
        recv[s, 0] = zero
        recv[s, depth + 1] = zero

    @pl.when(jnp.logical_not(has_prev))
    def _():
        recv[0] = jnp.zeros((depth + 2, frames, width), BF16)

    @pl.when(jnp.logical_not(has_next))
    def _():
        recv[1] = jnp.zeros((depth + 2, frames, width), BF16)

    def halo(side, c):
        zs = pl.ds(bounds[c] + 1, bounds[c + 1] - bounds[c])
        return pltpu.make_async_remote_copy(
            src_ref=vox.at[rows - 1 if side == 0 else 0, zs],
            dst_ref=recv.at[side, zs],
            send_sem=hsend_sem.at[side, c],
            recv_sem=hrecv_sem.at[side, c],
            device_id={"space": me + 1 if side == 0 else me - 1},
            device_id_type=MESH,
        )

    for c in range(chunks):
        loads[c].wait()

        for z in range(bounds[c], bounds[c + 1]):
            full = vid[:, z].astype(F32).reshape(total, width).astype(BF16)
            for b in range(blocks):
                turned = dot(turn, full[b * block:(b + 1) * block]).astype(BF16)
                for y in range(rows):
                    vox[y, z + 1, b * fb:(b + 1) * fb] = turned[y * fb:(y + 1) * fb]
        if c == 0:
            waits = has_prev.astype(jnp.int32) + has_next.astype(jnp.int32)
            pl.semaphore_wait(barrier, waits + (inner - 1) + (outer - 1))

        @pl.when(has_next)
        def _():
            halo(0, c).start()

        @pl.when(has_prev)
        def _():
            halo(1, c).start()

    def smooth_xz(field):
        flatter = field.reshape((depth + 2) * frames, width)
        x = dot(flatter, along).reshape(depth + 2, frames, width)
        return (x[:depth] + x[2:]) + 2.0 * x[1:depth + 1]

    def place(slot, y, smooth):
        high = (vox[y, pl.ds(1, depth)].astype(F32) - smooth).astype(BF16)
        base = slot * frames
        if not isinstance(slot, int):
            base = pl.multiple_of(base, frames)
        for z in range(depth):
            flat[pl.ds(base, frames), z * width:(z + 1) * width] = high[z]

    def gram_of(pair):
        base = pair * 2 * frames
        if not isinstance(pair, int):
            base = pl.multiple_of(base, 2 * frames)
        both = flat[pl.ds(base, 2 * frames), :]
        return lax.dot_general(
            both, both, (((1,), (1,)), ((), ())), preferred_element_type=F32
        )

    for y in range(rows):
        zsum[y] = smooth_xz(vox[y])
        if y >= 2:
            place(y - 2, y - 1, (zsum[y - 2] + zsum[y]) + 2.0 * zsum[y - 1])
    pairs = gram_of(0)
    for pair in range(1, rows // 2 - 1):
        pairs = pairs + gram_of(pair)
    acc[...] = pairs

    for c in range(chunks):
        @pl.when(has_next)
        def _():
            halo(1, c).wait_recv()
    place(rows - 2, rows - 1, (zsum[rows - 2] + smooth_xz(recv[1])) + 2.0 * zsum[rows - 1])
    for c in range(chunks):
        @pl.when(has_prev)
        def _():
            halo(0, c).wait_recv()
    place(rows - 1, 0, (smooth_xz(recv[0]) + zsum[1]) + 2.0 * zsum[0])

    half = frames // 2
    pairs = acc[...] + gram_of(rows // 2 - 1)
    whole = pairs[:frames] + pltpu.roll(pairs[frames:], frames, 1)
    whole = jnp.where(iota((frames, 2 * frames), 1) < frames, whole, 0.0)
    packed = whole[:half] + pltpu.roll(whole[half:], frames, 1)

    def exchange(value, slot, peers, recv_ref, ssem, rsem):
        gsend[slot] = value
        copies = []
        for d, peer in enumerate(peers):
            copies.append(pltpu.make_async_remote_copy(
                src_ref=gsend.at[slot], dst_ref=recv_ref.at[d],
                send_sem=ssem.at[d], recv_sem=rsem.at[d],
                device_id={"space": peer}, device_id_type=MESH,
            ))
            copies[-1].start()
        for d, copy in enumerate(copies):
            copy.wait_recv()
            value = value + recv_ref[d]
        return value, copies

    packed, copies1 = exchange(packed, 0, peers1, grecv1, g1s_sem, g1r_sem)
    packed, copies2 = exchange(packed, 1, peers2, grecv2, g2s_sem, g2r_sem)
    gram_out[...] = packed
    for copy in copies1 + copies2:
        copy.wait_send()
    for c in range(chunks):
        @pl.when(has_next)
        def _():
            halo(0, c).wait_send()

        @pl.when(has_prev)
        def _():
            halo(1, c).wait_send()


def filtered_gram(video, n):
    frames, depth, rows, width = video.shape
    total = frames * rows
    block = min(total, max(rows, (256 // rows) * rows))
    chunks = 4 if depth % 4 == 0 else 1
    inner = 4 if n % 4 == 0 else (2 if n % 2 == 0 else 1)
    outer = n // inner
    cfg = (n, inner, outer, frames, depth, rows, width, block, chunks)
    half = frames // 2
    dma = pltpu.SemaphoreType.DMA
    return pl.pallas_call(
        functools.partial(filter_kernel, cfg),
        out_shape=(
            jax.ShapeDtypeStruct((total, depth * width), BF16),
            jax.ShapeDtypeStruct((half, 2 * frames), F32),
        ),
        in_specs=[pl.BlockSpec(memory_space=pl.ANY)],
        out_specs=(
            pl.BlockSpec(memory_space=pltpu.VMEM),
            pl.BlockSpec(memory_space=pltpu.VMEM),
        ),
        scratch_shapes=[
            pltpu.VMEM((frames, depth, rows, width), BF16),
            pltpu.VMEM((rows, depth + 2, frames, width), BF16),
            pltpu.VMEM((rows, depth, frames, width), F32),
            pltpu.VMEM((2, depth + 2, frames, width), BF16),
            pltpu.VMEM((2 * frames, 2 * frames), F32),
            pltpu.VMEM((2, half, 2 * frames), F32),
            pltpu.VMEM((max(inner - 1, 1), half, 2 * frames), F32),
            pltpu.VMEM((max(outer - 1, 1), half, 2 * frames), F32),
            dma((chunks,)),
            dma((2, chunks)),
            dma((2, chunks)),
            dma((max(inner - 1, 1),)),
            dma((max(inner - 1, 1),)),
            dma((max(outer - 1, 1),)),
            dma((max(outer - 1, 1),)),
        ],
        compiler_params=pltpu.CompilerParams(
            collective_id=0, has_side_effects=True, vmem_limit_bytes=48 * 2**20
        ),
    )(video)


def remix_kernel(cfg, shrink, gram, flat, out, obuf, store_sem):
    frames, depth, rows, width, chunks = cfg
    bounds = chunk_bounds(depth, chunks)
    total, half, lanes = frames * rows, frames // 2, 2 * frames
    packed = gram[...]
    other = pltpu.roll(packed, frames, 1)
    r, c = iota((frames, lanes), 0), iota((frames, lanes), 1)
    whole = jnp.where(c < frames, jnp.concatenate([packed, other], axis=0), 0.0)
    eye = jnp.where(r == c, 1.0, 0.0)
    ridge = shrink[0] * jnp.sum(whole * eye) / frames
    system = whole + ridge * eye

    tiles = frames // 8
    parts = [system[8 * t:8 * t + 8] for t in range(tiles)]
    lane, sub = iota((8, lanes), 1), iota((8, lanes), 0)
    group = 4
    for k in range(0, frames, group):
        home, at = k // 8, k % 8
        span = range(group)
        cols = [[jnp.broadcast_to(p[:, k + i:k + i + 1], (8, lanes)) for p in parts] for i in span]
        line = [jnp.broadcast_to(parts[home][at + i:at + i + 1], (8, lanes)) for i in span]

        def splats(tile, rows_at, lanes_at):
            spread = [jnp.broadcast_to(tile[:, j:j + 1], (8, lanes)) for j in lanes_at]
            return {
                (i, j): jnp.broadcast_to(spread[j][at_row:at_row + 1], (8, lanes))
                for i, at_row in enumerate(rows_at) for j in span
            }

        here = [at + i for i in span]
        if k == 0:
            own = splats(parts[home], here, list(span))
        ahead = k + group
        if ahead < frames:
            there = [ahead + j for j in span]
            old = splats(parts[ahead // 8], [ahead % 8 + i for i in span], there)
            cross = splats(parts[home], here, there)

        def of(i, j):
            return own[max(i, j), min(i, j)]

        for q in span:
            inverse = recip(own[q, q])
            scaled = [of(i, q) * inverse for i in span]
            fresh = {}
            for i in span:
                for j in range(i + 1):
                    if i == q and j == q:
                        fresh[i, j] = -inverse
                    elif i == q:
                        fresh[i, j] = scaled[j]
                    elif j == q:
                        fresh[i, j] = scaled[i]
                    else:
                        fresh[i, j] = own[i, j] - of(i, q) * scaled[j]
            own = fresh
        wide = []
        for i in span:
            value = -sum(of(i, j) * line[j] for j in span)
            for j in span:
                value = jnp.where(lane == k + j, of(i, j), value)
            wide.append(value)
        if ahead < frames:
            gain = {
                (i, j): -sum(of(i, m) * cross[m, j] for m in span) for i in span for j in span
            }
            following = {
                (i, j): old[i, j] - sum(cross[m, i] * gain[m, j] for m in span)
                for i in span for j in range(i + 1)
            }
        inside = (lane >= k) & (lane < k + group)
        for t in range(tiles):
            terms = [cols[i][t] * wide[i] for i in span]
            while len(terms) > 1:
                terms = [a + b for a, b in zip(terms[::2], terms[1::2])]
            new = jnp.where(inside, 0.0, parts[t]) - terms[0]
            if t == home:
                for i in span:
                    new = jnp.where(sub == at + i, wide[i], new)
            parts[t] = new
        if ahead < frames:
            own = following
    mixing = (eye + ridge * jnp.concatenate(parts, axis=0)).astype(BF16)

    r, c = iota((total, frames), 0), iota((total, frames), 1)
    spread = jnp.where(r // rows == c, 1.0, 0.0).astype(BF16)
    tall = dot(spread, mixing).astype(BF16)
    r, c = iota((lanes, total), 0), iota((lanes, total), 1)
    spread = jnp.where(r == lax.rem(c, frames), 1.0, 0.0).astype(BF16)
    big = dot(tall, spread)
    keep = lax.rem(iota((total, total), 0), rows) == lax.rem(iota((total, total), 1) // frames + 1, rows)
    big = jnp.where(keep, big, 0.0).astype(BF16)

    stores = []
    for c in range(chunks):
        for z in range(bounds[c], bounds[c + 1]):
            value = dot(big, flat[:, z * width:(z + 1) * width])
            obuf[:, z] = value.reshape(frames, rows, width).astype(BF16)
        zs = pl.ds(bounds[c], bounds[c + 1] - bounds[c])
        stores.append(pltpu.make_async_copy(obuf.at[:, zs], out.at[:, zs], store_sem.at[c]))
        stores[-1].start()
    for store in stores:
        store.wait()


def remix(shrink, gram, flat, shape):
    frames, depth, rows, width = shape
    chunks = 4 if depth % 4 == 0 else 1
    cfg = (frames, depth, rows, width, chunks)
    return pl.pallas_call(
        functools.partial(remix_kernel, cfg),
        out_shape=jax.ShapeDtypeStruct(shape, BF16),
        in_specs=[
            pl.BlockSpec(memory_space=pltpu.SMEM),
            pl.BlockSpec(memory_space=pltpu.VMEM),
            pl.BlockSpec(memory_space=pltpu.VMEM),
        ],
        out_specs=pl.BlockSpec(memory_space=pl.ANY),
        scratch_shapes=[
            pltpu.VMEM(shape, BF16),
            pltpu.SemaphoreType.DMA((chunks,)),
        ],
        compiler_params=pltpu.CompilerParams(vmem_limit_bytes=32 * 2**20),
    )(shrink, gram, flat)


def per_device(n, video, shrink):
    flat, gram = filtered_gram(video, n)
    return remix(shrink, gram, flat, video.shape)


def solution(mesh):
    return jax.shard_map(
        functools.partial(per_device, mesh.shape["space"]),
        mesh=mesh,
        in_specs=(P(None, None, ("groups", "space"), None), P("groups")),
        out_specs=P(None, None, ("groups", "space"), None),
        check_vma=False,
    )
```

```python
import functools

import jax
import jax.numpy as jnp
from jax import lax
from jax.experimental import pallas as pl
from jax.experimental.pallas import tpu as pltpu
from jax.sharding import PartitionSpec as P

MESH = pl.DeviceIdType.MESH
F32 = jnp.float32
BF16 = jnp.bfloat16


def iota(shape, dim):
    return lax.broadcasted_iota(jnp.int32, shape, dim)


def recip(x):
    r = pl.reciprocal(x, approx=True)
    for _ in range(2):
        r = r * (2.0 - x * r)
    return r


def dot(a, b):
    return jnp.dot(a, b, preferred_element_type=F32)


def chunk_bounds(depth, chunks):
    return [depth * c // chunks for c in range(chunks + 1)]


def filter_kernel(
    cfg, video, flat, gram_out,
    vid, vox, zsum, recv, acc, gsend, grecv1, grecv2,
    load_sem, hsend_sem, hrecv_sem, g1s_sem, g1r_sem, g2s_sem, g2r_sem,
):
    n, inner, outer, frames, depth, rows, width, block, chunks = cfg
    me = lax.axis_index("space")
    bounds = chunk_bounds(depth, chunks)
    total = frames * rows
    blocks = total // block
    fb = block // rows
    has_prev, has_next = me > 0, me < n - 1

    loads = []
    for c in range(chunks):
        zs = pl.ds(bounds[c], bounds[c + 1] - bounds[c])
        loads.append(pltpu.make_async_copy(video.at[:, zs], vid.at[:, zs], load_sem.at[c]))
        loads[-1].start()

    pos, ring = lax.rem(me, inner), me // inner
    peers1 = [ring * inner + lax.rem(pos + d, inner) for d in range(1, inner)]
    peers2 = [lax.rem(ring + d, outer) * inner + pos for d in range(1, outer)]
    barrier = pltpu.get_barrier_semaphore()

    @pl.when(has_prev)
    def _():
        pl.semaphore_signal(barrier, inc=1, device_id={"space": me - 1}, device_id_type=MESH)

    @pl.when(has_next)
    def _():
        pl.semaphore_signal(barrier, inc=1, device_id={"space": me + 1}, device_id_type=MESH)

    for peer in peers1 + peers2:
        pl.semaphore_signal(barrier, inc=1, device_id={"space": peer}, device_id_type=MESH)

    r, c = iota((block, block), 0), iota((block, block), 1)
    turn = jnp.where(lax.rem(r, fb) * rows + r // fb == c, 1.0, 0.0).astype(BF16)
    r, c = iota((width, width), 0), iota((width, width), 1)
    step = r - c
    along = jnp.where(step == 0, 2.0, jnp.where((step == 1) | (step == -1), 1.0, 0.0))
    along = (along / 64.0).astype(BF16)

    zero = jnp.zeros((frames, width), BF16)
    for y in range(rows):
        vox[y, 0] = zero
        vox[y, depth + 1] = zero
    for s in range(2):
        recv[s, 0] = zero
        recv[s, depth + 1] = zero

    @pl.when(jnp.logical_not(has_prev))
    def _():
        recv[0] = jnp.zeros((depth + 2, frames, width), BF16)

    @pl.when(jnp.logical_not(has_next))
    def _():
        recv[1] = jnp.zeros((depth + 2, frames, width), BF16)

    def halo(side, c):
        zs = pl.ds(bounds[c] + 1, bounds[c + 1] - bounds[c])
        return pltpu.make_async_remote_copy(
            src_ref=vox.at[rows - 1 if side == 0 else 0, zs],
            dst_ref=recv.at[side, zs],
            send_sem=hsend_sem.at[side, c],
            recv_sem=hrecv_sem.at[side, c],
            device_id={"space": me + 1 if side == 0 else me - 1},
            device_id_type=MESH,
        )

    for c in range(chunks):
        loads[c].wait()

        for z in range(bounds[c], bounds[c + 1]):
            full = vid[:, z].astype(F32).reshape(total, width).astype(BF16)
            for b in range(blocks):
                turned = dot(turn, full[b * block:(b + 1) * block]).astype(BF16)
                for y in range(rows):
                    vox[y, z + 1, b * fb:(b + 1) * fb] = turned[y * fb:(y + 1) * fb]
        if c == 0:
            waits = has_prev.astype(jnp.int32) + has_next.astype(jnp.int32)
            pl.semaphore_wait(barrier, waits + (inner - 1) + (outer - 1))

        @pl.when(has_next)
        def _():
            halo(0, c).start()

        @pl.when(has_prev)
        def _():
            halo(1, c).start()

    def smooth_xz(field):
        deep = field.shape[0]
        x = dot(field.reshape(deep * frames, width), along).reshape(deep, frames, width)
        return (x[:deep - 2] + x[2:]) + 2.0 * x[1:deep - 1]

    def place(slot, y, smooth, lo=0, hi=depth):
        high = (vox[y, lo + 1:hi + 1].astype(F32) - smooth).astype(BF16)
        for z in range(lo, hi):
            flat[slot * frames:(slot + 1) * frames, z * width:(z + 1) * width] = high[z - lo]

    def gram_of(pair, lo=0, hi=depth):
        both = flat[pair * 2 * frames:(pair + 1) * 2 * frames, lo * width:hi * width]
        return lax.dot_general(
            both, both, (((1,), (1,)), ((), ())), preferred_element_type=F32
        )

    for y in range(rows):
        zsum[y] = smooth_xz(vox[y])
        if y >= 2:
            place(y - 2, y - 1, (zsum[y - 2] + zsum[y]) + 2.0 * zsum[y - 1])
    pairs = gram_of(0)
    for pair in range(1, rows // 2 - 1):
        pairs = pairs + gram_of(pair)
    acc[...] = pairs

    for c in range(chunks):
        @pl.when(has_next)
        def _():
            halo(1, c).wait_recv()

        @pl.when(has_prev)
        def _():
            halo(0, c).wait_recv()

        lo = bounds[c] - 1 if c else 0
        hi = bounds[c + 1] - 1 if c < chunks - 1 else depth
        after = smooth_xz(recv[1, lo:hi + 2])
        before = smooth_xz(recv[0, lo:hi + 2])
        last, first = rows - 1, 0
        place(rows - 2, last, (zsum[last - 1, lo:hi] + after) + 2.0 * zsum[last, lo:hi], lo, hi)
        place(rows - 1, first, (before + zsum[1, lo:hi]) + 2.0 * zsum[first, lo:hi], lo, hi)
        acc[...] += gram_of(rows // 2 - 1, lo, hi)

    half = frames // 2
    pairs = acc[...]
    whole = pairs[:frames] + pltpu.roll(pairs[frames:], frames, 1)
    whole = jnp.where(iota((frames, 2 * frames), 1) < frames, whole, 0.0)
    packed = whole[:half] + pltpu.roll(whole[half:], frames, 1)

    def exchange(value, slot, peers, recv_ref, ssem, rsem):
        gsend[slot] = value
        copies = []
        for d, peer in enumerate(peers):
            copies.append(pltpu.make_async_remote_copy(
                src_ref=gsend.at[slot], dst_ref=recv_ref.at[d],
                send_sem=ssem.at[d], recv_sem=rsem.at[d],
                device_id={"space": peer}, device_id_type=MESH,
            ))
            copies[-1].start()
        for d, copy in enumerate(copies):
            copy.wait_recv()
            value = value + recv_ref[d]
        return value, copies

    packed, copies1 = exchange(packed, 0, peers1, grecv1, g1s_sem, g1r_sem)
    packed, copies2 = exchange(packed, 1, peers2, grecv2, g2s_sem, g2r_sem)
    gram_out[...] = packed
    for copy in copies1 + copies2:
        copy.wait_send()
    for c in range(chunks):
        @pl.when(has_next)
        def _():
            halo(0, c).wait_send()

        @pl.when(has_prev)
        def _():
            halo(1, c).wait_send()


def filtered_gram(video, n):
    frames, depth, rows, width = video.shape
    total = frames * rows
    block = min(total, max(rows, (256 // rows) * rows))
    chunks = 4 if depth % 4 == 0 else 1
    inner = 4 if n % 4 == 0 else (2 if n % 2 == 0 else 1)
    outer = n // inner
    cfg = (n, inner, outer, frames, depth, rows, width, block, chunks)
    half = frames // 2
    dma = pltpu.SemaphoreType.DMA
    return pl.pallas_call(
        functools.partial(filter_kernel, cfg),
        out_shape=(
            jax.ShapeDtypeStruct((total, depth * width), BF16),
            jax.ShapeDtypeStruct((half, 2 * frames), F32),
        ),
        in_specs=[pl.BlockSpec(memory_space=pl.ANY)],
        out_specs=(
            pl.BlockSpec(memory_space=pltpu.VMEM),
            pl.BlockSpec(memory_space=pltpu.VMEM),
        ),
        scratch_shapes=[
            pltpu.VMEM((frames, depth, rows, width), BF16),
            pltpu.VMEM((rows, depth + 2, frames, width), BF16),
            pltpu.VMEM((rows, depth, frames, width), F32),
            pltpu.VMEM((2, depth + 2, frames, width), BF16),
            pltpu.VMEM((2 * frames, 2 * frames), F32),
            pltpu.VMEM((2, half, 2 * frames), F32),
            pltpu.VMEM((max(inner - 1, 1), half, 2 * frames), F32),
            pltpu.VMEM((max(outer - 1, 1), half, 2 * frames), F32),
            dma((chunks,)),
            dma((2, chunks)),
            dma((2, chunks)),
            dma((max(inner - 1, 1),)),
            dma((max(inner - 1, 1),)),
            dma((max(outer - 1, 1),)),
            dma((max(outer - 1, 1),)),
        ],
        compiler_params=pltpu.CompilerParams(
            collective_id=0, has_side_effects=True, vmem_limit_bytes=48 * 2**20
        ),
    )(video)


def remix_kernel(cfg, shrink, gram, flat, out, obuf, store_sem):
    frames, depth, rows, width, chunks = cfg
    bounds = chunk_bounds(depth, chunks)
    total, half, lanes = frames * rows, frames // 2, 2 * frames
    packed = gram[...]
    other = pltpu.roll(packed, frames, 1)
    r, c = iota((frames, lanes), 0), iota((frames, lanes), 1)
    whole = jnp.where(c < frames, jnp.concatenate([packed, other], axis=0), 0.0)
    eye = jnp.where(r == c, 1.0, 0.0)
    ridge = shrink[0] * jnp.sum(whole * eye) / frames
    system = whole + ridge * eye

    tiles = frames // 8
    parts = [system[8 * t:8 * t + 8] for t in range(tiles)]
    lane, sub = iota((8, lanes), 1), iota((8, lanes), 0)
    group = 4
    for k in range(0, frames, group):
        home, at = k // 8, k % 8
        span = range(group)
        cols = [[jnp.broadcast_to(p[:, k + i:k + i + 1], (8, lanes)) for p in parts] for i in span]
        line = [jnp.broadcast_to(parts[home][at + i:at + i + 1], (8, lanes)) for i in span]

        def splats(tile, rows_at, lanes_at):
            spread = [jnp.broadcast_to(tile[:, j:j + 1], (8, lanes)) for j in lanes_at]
            return {
                (i, j): jnp.broadcast_to(spread[j][at_row:at_row + 1], (8, lanes))
                for i, at_row in enumerate(rows_at) for j in span
            }

        here = [at + i for i in span]
        if k == 0:
            own = splats(parts[home], here, list(span))
        ahead = k + group
        if ahead < frames:
            there = [ahead + j for j in span]
            old = splats(parts[ahead // 8], [ahead % 8 + i for i in span], there)
            cross = splats(parts[home], here, there)

        def of(i, j):
            return own[max(i, j), min(i, j)]

        for q in span:
            inverse = recip(own[q, q])
            scaled = [of(i, q) * inverse for i in span]
            fresh = {}
            for i in span:
                for j in range(i + 1):
                    if i == q and j == q:
                        fresh[i, j] = -inverse
                    elif i == q:
                        fresh[i, j] = scaled[j]
                    elif j == q:
                        fresh[i, j] = scaled[i]
                    else:
                        fresh[i, j] = own[i, j] - of(i, q) * scaled[j]
            own = fresh
        wide = []
        for i in span:
            value = -sum(of(i, j) * line[j] for j in span)
            for j in span:
                value = jnp.where(lane == k + j, of(i, j), value)
            wide.append(value)
        if ahead < frames:
            gain = {
                (i, j): -sum(of(i, m) * cross[m, j] for m in span) for i in span for j in span
            }
            following = {
                (i, j): old[i, j] - sum(cross[m, i] * gain[m, j] for m in span)
                for i in span for j in range(i + 1)
            }
        inside = (lane >= k) & (lane < k + group)
        for t in range(tiles):
            terms = [cols[i][t] * wide[i] for i in span]
            while len(terms) > 1:
                terms = [a + b for a, b in zip(terms[::2], terms[1::2])]
            new = jnp.where(inside, 0.0, parts[t]) - terms[0]
            if t == home:
                for i in span:
                    new = jnp.where(sub == at + i, wide[i], new)
            parts[t] = new
        if ahead < frames:
            own = following
    mixing = (eye + ridge * jnp.concatenate(parts, axis=0)).astype(BF16)

    r, c = iota((total, frames), 0), iota((total, frames), 1)
    spread = jnp.where(r // rows == c, 1.0, 0.0).astype(BF16)
    tall = dot(spread, mixing).astype(BF16)
    r, c = iota((lanes, total), 0), iota((lanes, total), 1)
    spread = jnp.where(r == lax.rem(c, frames), 1.0, 0.0).astype(BF16)
    big = dot(tall, spread)
    keep = lax.rem(iota((total, total), 0), rows) == lax.rem(iota((total, total), 1) // frames + 1, rows)
    big = jnp.where(keep, big, 0.0).astype(BF16)

    stores = []
    for c in range(chunks):
        for z in range(bounds[c], bounds[c + 1]):
            value = dot(big, flat[:, z * width:(z + 1) * width])
            obuf[:, z] = value.reshape(frames, rows, width).astype(BF16)
        zs = pl.ds(bounds[c], bounds[c + 1] - bounds[c])
        stores.append(pltpu.make_async_copy(obuf.at[:, zs], out.at[:, zs], store_sem.at[c]))
        stores[-1].start()
    for store in stores:
        store.wait()


def remix(shrink, gram, flat, shape):
    frames, depth, rows, width = shape
    chunks = 4 if depth % 4 == 0 else 1
    cfg = (frames, depth, rows, width, chunks)
    return pl.pallas_call(
        functools.partial(remix_kernel, cfg),
        out_shape=jax.ShapeDtypeStruct(shape, BF16),
        in_specs=[
            pl.BlockSpec(memory_space=pltpu.SMEM),
            pl.BlockSpec(memory_space=pltpu.VMEM),
            pl.BlockSpec(memory_space=pltpu.VMEM),
        ],
        out_specs=pl.BlockSpec(memory_space=pl.ANY),
        scratch_shapes=[
            pltpu.VMEM(shape, BF16),
            pltpu.SemaphoreType.DMA((chunks,)),
        ],
        compiler_params=pltpu.CompilerParams(vmem_limit_bytes=32 * 2**20),
    )(shrink, gram, flat)


def per_device(n, video, shrink):
    flat, gram = filtered_gram(video, n)
    return remix(shrink, gram, flat, video.shape)


def solution(mesh):
    return jax.shard_map(
        functools.partial(per_device, mesh.shape["space"]),
        mesh=mesh,
        in_specs=(P(None, None, ("groups", "space"), None), P("groups")),
        out_specs=P(None, None, ("groups", "space"), None),
        check_vma=False,
    )
```
